256 devices in a mesh: row: 16 (over y, x_hi, core), col: 16 (over z, x_lo).
Axes of the slice: x: 4 (x_hi: 2, x_lo: 2; x = x_hi * 2 + x_lo), y: 4, z: 8, core: 2. Of those that a mesh axis runs over, the one named last changes fastest.
Arguments:
- trials: float32 [2, 512, 1024], P(None, 'col', 'row'), may hold values from -6 to 6
- valence_factor: float32 [16384, 512], P('row'), may hold values from -0.25 to 0.25
- conduction_factor: float32 [16384, 1024], P('col', 'row'), may hold values from -0.046875 to 0.046875
- screened: float32 [16384, 16384], P('row', 'col'), may hold values from -6 to 6
- valence_energy: float32 [512], P('col'), may hold values from -0.6 to -0.1
- conduction_energy: float32 [1024], P('row'), may hold values from 0.1 to 0.6
Outputs:
- applied: float32 [2, 512, 1024], P(None, 'col', 'row')
The draws below stay inside these ranges and needn't reach their ends.
All inputs are finite; a program needn't handle non-finite values.
Results may differ from the reference program's by a relative error of at most 0.0001.
Values sent between devices are 32-bit elements; how exact they have to be, the bound alone decides.
No kernel may reach another device: no remote copies, remote signals or barrier semaphores. Data moves between devices by JAX's collectives and lax.ppermute only.
A program may use at most 64 MiB of HBM per device.

```python
import jax
import jax.numpy as jnp
from jax import lax

V = 512
C = 1024
NP = 16384
B = 2


def steps_of(stream_key, shape, pieces, smallest, largest):
    def one(dim, blocks):
        steps = jax.random.uniform(jax.random.fold_in(jax.random.fold_in(stream_key, 6), dim), (blocks,), jnp.float32, smallest / len(pieces), largest / len(pieces))
        return jnp.repeat(jnp.exp(steps), shape[dim] // blocks).reshape((-1,) + (1,) * (len(shape) - dim - 1))

    loudness = one(*pieces[0])
    for cut in pieces[1:]:
        loudness = loudness * one(*cut)
    return loudness


def normal_values(own_key, shape, spread, bound, pieces=(), dtype=jnp.bfloat16):
    values = jax.random.normal(own_key, shape, jnp.float32) * spread
    if len(pieces) > 0:
        values = steps_of(own_key, shape, pieces, -0.22, 0.18) * values
    return jnp.clip(values, min=-bound, max=bound).astype(dtype)


def setup_inputs(seed: int = 0) -> dict:
    seeds = jax.random.split(jax.random.key(seed), 7)
    return {
        "trials": normal_values(seeds[0], (B, V, C), 1.0, 6.0, ((1, 16), (2, 16)), jnp.float32),
        "valence_factor": normal_values(seeds[1], (NP, V), V ** -0.5, 0.25, ((0, 16),), jnp.float32),
        "conduction_factor": normal_values(seeds[2], (NP, C), NP ** -0.5, 0.046875, ((0, 16), (1, 16)), jnp.float32),
        "screened": normal_values(seeds[3], (NP, NP), 1.0, 6.0, ((0, 16), (1, 16)), jnp.float32),
        "valence_energy": jnp.clip(-0.6 + 0.5 * jax.random.uniform(seeds[4], (V,), jnp.float32) ** steps_of(seeds[4], (V,), ((0, 16),), -0.2, 0.2), -0.6, -0.1),
        "conduction_energy": jnp.clip(0.1 + 0.5 * jax.random.uniform(seeds[5], (C,), jnp.float32) ** steps_of(seeds[5], (C,), ((0, 16),), -0.2, 0.2), 0.1, 0.6),
    }


def reference(trials, valence_factor, conduction_factor, screened, valence_energy, conduction_energy):
    highest = lax.Precision.HIGHEST
    points = jnp.einsum('bvc,nc->bvn', trials, conduction_factor, precision=highest)
    blocks = 16
    block_rows = NP // blocks
    valence_blocks = valence_factor.reshape(blocks, block_rows, V)
    screened_blocks = screened.reshape(blocks, block_rows, NP)

    def accumulate(total, item):
        valence_piece, screened_piece = item
        expanded = jnp.einsum('mv,bvn->bmn', valence_piece, points, precision=highest)
        weighted = expanded * screened_piece[None]
        return total + jnp.einsum('mv,bmn->bvn', valence_piece, weighted, precision=highest), None

    folded, unused = lax.scan(accumulate, jnp.zeros((B, V, NP), jnp.float32), (valence_blocks, screened_blocks))
    kernel_term = jnp.einsum('bvn,nc->bvc', folded, conduction_factor, precision=highest)
    differences = conduction_energy[None, :] - valence_energy[:, None]
    return differences[None] * trials - kernel_term
```

```python
import jax
import jax.numpy as jnp
from jax import lax
from jax.sharding import PartitionSpec as P

CHIPS = ((0, 0), (1, 0), (3, 0), (2, 0), (0, 1), (1, 1), (3, 1), (2, 1))


def along_row(value, dy, dx, flip=0):
    pairs = [
        (i, ((i // 4 + dy) % 4) * 4 + ((i // 2 % 2) ^ dx) * 2 + ((i % 2) ^ flip)) for i in range(16)
    ]
    return lax.ppermute(value, "row", pairs)


def along_col(value, dz, dx):
    pairs = [(j, ((j // 2 + dz) % 8) * 2 + ((j % 2) ^ dx)) for j in range(16)]
    return lax.ppermute(value, "col", pairs)


def body(trials, valence_factor, conduction_factor, screened, valence_energy, conduction_energy):
    high = lax.Precision.HIGH
    col = lax.axis_index("col")
    z, x_lo = col // 2, col % 2
    rows = valence_factor.shape[0]

    with jax.named_scope("gather_trials_row"):
        own = jnp.concatenate(
            [trials if r == (0, 0) else along_row(trials, *r) for r in CHIPS], axis=2
        )
    with jax.named_scope("gather_conduction"):
        piece = conduction_factor.T
        mine = jnp.concatenate(
            [piece if r == (0, 0) else along_row(piece, *r) for r in CHIPS], axis=0
        )
        other = along_row(mine, 0, 0, 1)
    with jax.named_scope("gather_trials_col"):
        up, down = [own], [own]
        for step in range(3):
            up.append(along_col(up[-1], 1, 0))
            down.append(along_col(down[-1], -1, 0))
        far = jnp.concatenate(
            [along_col(up[-1][:1], 1, 0), along_col(down[-1][1:], -1, 0)], axis=0
        )
        blocks = [own, down[1], down[2], down[3], far, up[3], up[2], up[1]]
        blocks = blocks + [along_col(block, 0, 1) for block in blocks]
        trials_mine = jnp.concatenate(blocks, axis=1)
        trials_other = along_row(trials_mine, 0, 0, 1)

    with jax.named_scope("order_valence"):
        valence = valence_factor.reshape(rows, 8, 2, 32)
        valence = jnp.roll(valence, -z, axis=1)
        valence = jnp.where(x_lo == 0, valence, valence[:, :, ::-1])
        valence = valence.transpose(0, 2, 1, 3).reshape(rows, 512)

    with jax.named_scope("points"):
        points = jnp.einsum("bvc,cn->bvn", trials_mine, mine, precision=high)
        points = points + jnp.einsum("bvc,cn->bvn", trials_other, other, precision=high)
    with jax.named_scope("screen"):
        expanded = jnp.einsum("mv,bvn->bmn", valence, points, precision=high)
        weighted = expanded * screened[None]
        folded = jnp.einsum("mv,bmn->bvn", valence, weighted, precision=high)
    with jax.named_scope("kernel_part"):
        part_other = jnp.einsum("cn,bvn->cbv", other, folded, precision=high).reshape(512, 1024)
        part_mine = jnp.einsum("cn,bvn->cbv", mine, folded, precision=high).reshape(512, 1024)
    with jax.named_scope("reduce_row"):
        part = part_mine + along_row(part_other, 0, 0, 1)
        part = part.reshape(8, 64, 1024)
        total = part[0]
        for k, (dy, dx) in enumerate(CHIPS):
            if k > 0:
                total = total + along_row(part[k], -dy, dx)
    with jax.named_scope("reduce_col"):
        total = total.reshape(64, 2, 2, 256)
        total = total[:, :, 0] + along_col(total[:, :, 1], 0, 1)
        total = total.reshape(64, 2, 8, 32).transpose(2, 3, 1, 0).reshape(8, 32, 128)
        term = total[0]
        for k in range(1, 8):
            term = term + along_col(total[k], k, 0)
        kernel_term = term.reshape(32, 2, 64).transpose(1, 0, 2)
    differences = conduction_energy[None, :] - valence_energy[:, None]
    return differences[None] * trials - kernel_term


def solution(mesh):
    in_specs = (
        P(None, "col", "row"),
        P("row", None),
        P("col", "row"),
        P("row", "col"),
        P("col"),
        P("row"),
    )
    out_specs = P(None, "col", "row")
    return jax.shard_map(body, mesh=mesh, in_specs=in_specs, out_specs=out_specs, check_vma=False)
```

```python
import functools

import jax
import jax.numpy as jnp
from jax import lax
from jax.experimental import pallas as pl
from jax.experimental.pallas import tpu as pltpu
from jax.sharding import Mesh, PartitionSpec as P

F32, BF16 = jnp.float32, jnp.bfloat16
NN = (((1,), (0,)), ((), ()))
NT = (((1,), (1,)), ((), ()))
ROW, COL = ("y", "xh", "core"), ("z", "xl")


def swap_core(value):
    return lax.ppermute(value, "core", [(0, 1), (1, 0)])


def along_y(value, step):
    return lax.ppermute(value, "y", [(i, (i + step) % 4) for i in range(4)])


def along_z(value, step):
    return lax.ppermute(value, "z", [(i, (i + step) % 8) for i in range(8)])


def exchange(value, axes):
    return lax.all_to_all(value, axes, 0, 0, tiled=True)


def split(value):
    high = value.astype(BF16)
    return high, (value - high.astype(F32)).astype(BF16)


def product(a, b, dims):
    def dot(x, y):
        return lax.dot_general(x, y, dims, preferred_element_type=F32)

    return dot(a[0], b[0]) + (dot(a[0], b[1]) + dot(a[1], b[0]))


def apply_kernel(place_ref, *refs):
    trials, blocks, refs = refs[:16], refs[16:24], refs[24:]
    valence, scr, out_m, out_o, x, c, va, s, sem_x, sem_c, sem_v = refs
    y, xh, z = place_ref[0], place_ref[1], place_ref[2]
    half, v = 512, 512
    points = scr.shape[1]

    copies_x = [
        [
            pltpu.make_async_copy(
                trials[8 * core + k].at[b],
                x.at[b, core, pl.ds(pl.multiple_of((z + k) % 8 * 64, 64), 64)],
                sem_x.at[b, core, k],
            )
            for core in range(2)
            for k in range(8)
        ]
        for b in range(2)
    ]
    copies_c = [
        pltpu.make_async_copy(
            blocks[4 * core + k].at[r], c.at[core, (y + k) % 4, (xh + r) % 2], sem_c.at[core, 2 * k + r]
        )
        for core in range(2)
        for k in range(4)
        for r in range(2)
    ]
    copy_v = pltpu.make_async_copy(valence, va, sem_v.at[0])
    copy_s = pltpu.make_async_copy(scr, s, sem_v.at[1])
    for copy in [copy_v] + copies_x[0] + copies_c + [copy_s] + copies_x[1]:
        copy.start()
    copy_v.wait()
    vector, transposed = split(va[...]), split(va[...].T)
    for copy in copies_c:
        copy.wait()
    conduction = [split(c[core].reshape(half, points)) for core in range(2)]
    for b in range(2):
        for copy in copies_x[b]:
            copy.wait()
        p = split(sum(product(split(x[b, core]), conduction[core], NN) for core in range(2)))
        e = product(vector, p, NN)
        if b == 0:
            copy_s.wait()
        w = split(e * s[...])
        f = split(product(transposed, w, NN))
        out_m[:, b] = product(conduction[0], f, NT).reshape(8, 64, v)
        out_o[:, b] = product(conduction[1], f, NT).reshape(8, 64, v)


def apply_both(place, gathered, blocks, valence, screened):
    rows, points = screened.shape
    half, v = 512, 512
    out = jax.ShapeDtypeStruct((8, 2, 64, v), F32)
    return pl.pallas_call(
        apply_kernel,
        out_shape=[out, out],
        in_specs=[pl.BlockSpec(memory_space=pltpu.SMEM)] + [pl.BlockSpec(memory_space=pltpu.HBM)] * 26,
        out_specs=[pl.BlockSpec(memory_space=pltpu.VMEM)] * 2,
        scratch_shapes=[
            pltpu.VMEM((2, 2, v, half), F32),
            pltpu.VMEM((2, 4, 2, 64, points), F32),
            pltpu.VMEM((rows, v), F32),
            pltpu.VMEM((rows, points), F32),
            pltpu.SemaphoreType.DMA((2, 2, 8)),
            pltpu.SemaphoreType.DMA((2, 8)),
            pltpu.SemaphoreType.DMA((2,)),
        ],
        compiler_params=pltpu.CompilerParams(vmem_limit_bytes=58 << 20),
        cost_estimate=pl.CostEstimate(flops=1024, bytes_accessed=1024, transcendentals=0),
    )(place, *gathered, *blocks, valence, screened)


def body(trials, valence_factor, conduction_factor, screened, valence_energy, conduction_energy):
    place = jnp.stack([lax.axis_index("y"), lax.axis_index("xh"), lax.axis_index("z")])

    with jax.named_scope("gather_conduction"):
        piece = conduction_factor.T
        pair = jnp.stack([piece, lax.ppermute(piece, "xh", [(0, 1), (1, 0)])])
    with jax.named_scope("gather_trials_plane"):
        plane = exchange(jnp.broadcast_to(trials.reshape(1, 32, 128), (16, 32, 128)), ("y", "xh", "xl"))
        plane = plane.reshape(8, 2, 2, 32, 64).transpose(2, 1, 3, 0, 4).reshape(2, 64, 512)
    with jax.named_scope("gather_conduction"):
        plane, pair = lax.optimization_barrier((plane, pair))
        turned = [along_y(pair, 3), along_y(pair, 2), along_y(pair, 1)]
    with jax.named_scope("gather_trials_z"):
        up, down = [plane], [plane]
        for step in range(3):
            up.append(along_z(up[-1], 1))
            down.append(along_z(down[-1], -1))
        up[3], down[3], *turned = lax.optimization_barrier((up[3], down[3], *turned))
        far = jnp.concatenate([along_z(up[-1][:1], 1), along_z(down[-1][1:], -1)], axis=0)
        gathered = [plane, down[1], down[2], down[3], far, up[3], up[2], up[1]]
        gathered = gathered + [swap_core(block) for block in gathered]
    with jax.named_scope("gather_conduction"):
        blocks = [pair, *turned]
        blocks = blocks + [swap_core(block) for block in blocks]

    with jax.named_scope("apply"):
        part, rest = apply_both(place, gathered, blocks, valence_factor, screened)
    with jax.named_scope("reduce_row"):
        total = exchange(part + swap_core(rest), ("y", "xh")).sum(axis=0)
    with jax.named_scope("reduce_col"):
        total = total.reshape(2, 64, 16, 32).transpose(2, 3, 0, 1).reshape(16, 32, 128)
        term = exchange(total, COL).sum(axis=0)
        kernel_term = term.reshape(32, 2, 64).transpose(1, 0, 2)
    differences = conduction_energy[None, :] - valence_energy[:, None]
    return differences[None] * trials - kernel_term


def solution(mesh):
    grid = Mesh(mesh.devices.reshape(4, 2, 2, 8, 2), ROW + COL)
    in_specs = (
        P(None, COL, ROW),
        P(ROW, None),
        P(COL, ROW),
        P(ROW, COL),
        P(COL),
        P(ROW),
    )
    out_specs = P(None, COL, ROW)
    return jax.shard_map(body, mesh=grid, in_specs=in_specs, out_specs=out_specs, check_vma=False)
```

```python
import functools

import jax
import jax.numpy as jnp
from jax import lax
from jax.experimental import pallas as pl
from jax.experimental.pallas import tpu as pltpu
from jax.sharding import Mesh, PartitionSpec as P

F32, BF16 = jnp.float32, jnp.bfloat16
NN = (((1,), (0,)), ((), ()))
NT = (((1,), (1,)), ((), ()))
ROW, COL = ("y", "xh", "core"), ("z", "xl")


def swap_core(value):
    return lax.ppermute(value, "core", [(0, 1), (1, 0)])


def along_y(value, step):
    return lax.ppermute(value, "y", [(i, (i + step) % 4) for i in range(4)])


def along_z(value, step):
    return lax.ppermute(value, "z", [(i, (i + step) % 8) for i in range(8)])


def exchange(value, axes):
    return lax.all_to_all(value, axes, 0, 0, tiled=True)


def split(value):
    high = value.astype(BF16)
    return high, (value - high.astype(F32)).astype(BF16)


def product(a, b, dims):
    def dot(x, y):
        return lax.dot_general(x, y, dims, preferred_element_type=F32)

    return dot(a[0], b[0]) + (dot(a[0], b[1]) + dot(a[1], b[0]))


def apply_kernel(place_ref, *refs):
    trials, blocks, refs = refs[:16], refs[16:24], refs[24:]
    valence, scr, *outs = refs[:6]
    x, c, va, s, sem_x, sem_c, sem_v = refs[6:]
    y, xh, z = place_ref[0], place_ref[1], place_ref[2]
    half, v = 512, 512
    points = scr.shape[1]

    copies_x = [
        [
            pltpu.make_async_copy(
                trials[8 * core + k].at[b],
                x.at[b, core, pl.ds(pl.multiple_of((z + k) % 8 * 64, 64), 64)],
                sem_x.at[b, core, k],
            )
            for core in range(2)
            for k in range(8)
        ]
        for b in range(2)
    ]
    copies_c = [
        pltpu.make_async_copy(
            blocks[4 * core + k].at[r], c.at[core, (y + k) % 4, (xh + r) % 2], sem_c.at[core, 2 * k + r]
        )
        for core in range(2)
        for k in range(4)
        for r in range(2)
    ]
    copy_v = pltpu.make_async_copy(valence, va, sem_v.at[0])
    copy_s = pltpu.make_async_copy(scr, s, sem_v.at[1])
    for copy in [copy_v] + copies_x[0] + copies_c + [copy_s] + copies_x[1]:
        copy.start()
    copy_v.wait()
    vector, transposed = split(va[...]), split(va[...].T)
    for copy in copies_c:
        copy.wait()
    conduction = [split(c[core].reshape(half, points)) for core in range(2)]
    for b in range(2):
        for copy in copies_x[b]:
            copy.wait()
        p = split(sum(product(split(x[b, core]), conduction[core], NN) for core in range(2)))
        e = product(vector, p, NN)
        if b == 0:
            copy_s.wait()
        w = split(e * s[...])
        f = split(product(transposed, w, NN))
        for core in range(2):
            outs[2 * core + b][...] = product(conduction[core], f, NT).reshape(8, 64, v)


def apply_both(place, gathered, blocks, valence, screened):
    rows, points = screened.shape
    half, v = 512, 512
    out = jax.ShapeDtypeStruct((8, 64, v), F32)
    return pl.pallas_call(
        apply_kernel,
        out_shape=[out] * 4,
        in_specs=[pl.BlockSpec(memory_space=pltpu.SMEM)] + [pl.BlockSpec(memory_space=pltpu.HBM)] * 26,
        out_specs=[pl.BlockSpec(memory_space=pltpu.VMEM)] * 4,
        scratch_shapes=[
            pltpu.VMEM((2, 2, v, half), F32),
            pltpu.VMEM((2, 4, 2, 64, points), F32),
            pltpu.VMEM((rows, v), F32),
            pltpu.VMEM((rows, points), F32),
            pltpu.SemaphoreType.DMA((2, 2, 8)),
            pltpu.SemaphoreType.DMA((2, 8)),
            pltpu.SemaphoreType.DMA((2,)),
        ],
        compiler_params=pltpu.CompilerParams(vmem_limit_bytes=58 << 20),
        cost_estimate=pl.CostEstimate(flops=1024, bytes_accessed=1024, transcendentals=0),
    )(place, *gathered, *blocks, valence, screened)


def body(trials, valence_factor, conduction_factor, screened, valence_energy, conduction_energy):
    place = jnp.stack([lax.axis_index("y"), lax.axis_index("xh"), lax.axis_index("z")])

    with jax.named_scope("gather_conduction"):
        piece = conduction_factor.T
        pair = jnp.stack([piece, lax.ppermute(piece, "xh", [(0, 1), (1, 0)])])
    with jax.named_scope("gather_trials_plane"):
        plane = exchange(jnp.broadcast_to(trials.reshape(1, 32, 128), (16, 32, 128)), ("y", "xh", "xl"))
        plane = plane.reshape(8, 2, 2, 32, 64).transpose(2, 1, 3, 0, 4).reshape(2, 64, 512)
    with jax.named_scope("gather_conduction"):
        plane, pair = lax.optimization_barrier((plane, pair))
        turned = [along_y(pair, 3), along_y(pair, 2), along_y(pair, 1)]
    with jax.named_scope("gather_trials_z"):
        up, down = [plane], [plane]
        for step in range(3):
            up.append(along_z(up[-1], 1))
            down.append(along_z(down[-1], -1))
        up[3], down[3], *turned = lax.optimization_barrier((up[3], down[3], *turned))
        far = jnp.concatenate([along_z(up[3][:1], 1), along_z(down[3][1:], -1)], axis=0)
        gathered = [plane, down[1], down[2], down[3], far, up[3], up[2], up[1]]
        gathered = gathered + [swap_core(block) for block in gathered]
    with jax.named_scope("gather_conduction"):
        blocks = [pair, *turned]
        blocks = blocks + [swap_core(block) for block in blocks]

    with jax.named_scope("apply"):
        pieces = apply_both(place, gathered, blocks, valence_factor, screened)
    with jax.named_scope("reduce_row"):
        pieces = [part + swap_core(rest) for part, rest in zip(pieces[:2], pieces[2:])]
        total = exchange(jnp.stack(pieces, axis=1), ("y", "xh")).sum(axis=0)
    with jax.named_scope("reduce_col"):
        total = total.reshape(2, 64, 16, 32).transpose(2, 3, 0, 1).reshape(16, 32, 128)
        term = exchange(total, COL).sum(axis=0)
        kernel_term = term.reshape(32, 2, 64).transpose(1, 0, 2)
    differences = conduction_energy[None, :] - valence_energy[:, None]
    return differences[None] * trials - kernel_term


def solution(mesh):
    grid = Mesh(mesh.devices.reshape(4, 2, 2, 8, 2), ROW + COL)
    in_specs = (
        P(None, COL, ROW),
        P(ROW, None),
        P(COL, ROW),
        P(ROW, COL),
        P(COL),
        P(ROW),
    )
    out_specs = P(None, COL, ROW)
    return jax.shard_map(body, mesh=grid, in_specs=in_specs, out_specs=out_specs, check_vma=False)
```

```python
import functools

import jax
import jax.numpy as jnp
from jax import lax
from jax.experimental import pallas as pl
from jax.experimental.pallas import tpu as pltpu
from jax.sharding import Mesh, PartitionSpec as P

F32, BF16 = jnp.float32, jnp.bfloat16
NN = (((1,), (0,)), ((), ()))
NT = (((1,), (1,)), ((), ()))
ROW, COL = ("y", "xh", "core"), ("z", "xl")


def swap_core(value):
    return lax.ppermute(value, "core", [(0, 1), (1, 0)])


def along_y(value, step):
    return lax.ppermute(value, "y", [(i, (i + step) % 4) for i in range(4)])


def along_z(value, step):
    return lax.ppermute(value, "z", [(i, (i + step) % 8) for i in range(8)])


def exchange(value, axes):
    return lax.all_to_all(value, axes, 0, 0, tiled=True)


def split(value):
    high = value.astype(BF16)
    return high, (value - high.astype(F32)).astype(BF16)


def product(a, b, dims):
    def dot(x, y):
        return lax.dot_general(x, y, dims, preferred_element_type=F32)

    return dot(a[0], b[0]) + (dot(a[0], b[1]) + dot(a[1], b[0]))


def apply_kernel(place_ref, *refs):
    trials, blocks, refs = refs[:18], refs[18:26], refs[26:]
    valence, scr, *outs = refs[:6]
    x, c, va, s, sem_x, sem_c, sem_v = refs[6:]
    y, xh, z = place_ref[0], place_ref[1], place_ref[2]
    half, v = 512, 512
    points = scr.shape[1]

    copies_x = [
        [
            pltpu.make_async_copy(
                trials[9 * core + 8].at[0] if (b, k) == (1, 4) else trials[9 * core + k].at[b],
                x.at[b, core, pl.ds(pl.multiple_of((z + k) % 8 * 64, 64), 64)],
                sem_x.at[b, core, k],
            )
            for core in range(2)
            for k in range(8)
        ]
        for b in range(2)
    ]
    copies_c = [
        pltpu.make_async_copy(
            blocks[4 * core + k].at[r], c.at[core, (y + k) % 4, (xh + r) % 2], sem_c.at[core, 2 * k + r]
        )
        for core in range(2)
        for k in range(4)
        for r in range(2)
    ]
    copy_v = pltpu.make_async_copy(valence, va, sem_v.at[0])
    copy_s = pltpu.make_async_copy(scr, s, sem_v.at[1])
    for copy in [copy_v] + copies_x[0] + copies_c + [copy_s] + copies_x[1]:
        copy.start()
    copy_v.wait()
    vector, transposed = split(va[...]), split(va[...].T)
    for copy in copies_c:
        copy.wait()
    conduction = [split(c[core].reshape(half, points)) for core in range(2)]
    for b in range(2):
        for copy in copies_x[b]:
            copy.wait()
        p = split(sum(product(split(x[b, core]), conduction[core], NN) for core in range(2)))
        e = product(vector, p, NN)
        if b == 0:
            copy_s.wait()
        w = split(e * s[...])
        f = split(product(transposed, w, NN))
        for core in range(2):
            outs[2 * core + b][...] = product(conduction[core], f, NT).reshape(8, 64, v)


def apply_both(place, gathered, blocks, valence, screened):
    rows, points = screened.shape
    half, v = 512, 512
    out = jax.ShapeDtypeStruct((8, 64, v), F32)
    return pl.pallas_call(
        apply_kernel,
        out_shape=[out] * 4,
        in_specs=[pl.BlockSpec(memory_space=pltpu.SMEM)] + [pl.BlockSpec(memory_space=pltpu.HBM)] * 28,
        out_specs=[pl.BlockSpec(memory_space=pltpu.VMEM)] * 4,
        scratch_shapes=[
            pltpu.VMEM((2, 2, v, half), F32),
            pltpu.VMEM((2, 4, 2, 64, points), F32),
            pltpu.VMEM((rows, v), F32),
            pltpu.VMEM((rows, points), F32),
            pltpu.SemaphoreType.DMA((2, 2, 8)),
            pltpu.SemaphoreType.DMA((2, 8)),
            pltpu.SemaphoreType.DMA((2,)),
        ],
        compiler_params=pltpu.CompilerParams(vmem_limit_bytes=58 << 20),
        cost_estimate=pl.CostEstimate(flops=1024, bytes_accessed=1024, transcendentals=0),
    )(place, *gathered, *blocks, valence, screened)


def body(trials, valence_factor, conduction_factor, screened, valence_energy, conduction_energy):
    place = jnp.stack([lax.axis_index("y"), lax.axis_index("xh"), lax.axis_index("z")])

    with jax.named_scope("gather_conduction"):
        piece = conduction_factor.T
        pair = jnp.stack([piece, lax.ppermute(piece, "xh", [(0, 1), (1, 0)])])
    with jax.named_scope("gather_trials_plane"):
        plane = exchange(jnp.broadcast_to(trials.reshape(1, 32, 128), (16, 32, 128)), ("y", "xh", "xl"))
        plane = plane.reshape(8, 2, 2, 32, 64).transpose(2, 1, 3, 0, 4).reshape(2, 64, 512)
    with jax.named_scope("gather_conduction"):
        plane, pair = lax.optimization_barrier((plane, pair))
        turned = [along_y(pair, 3), along_y(pair, 2), along_y(pair, 1)]
    with jax.named_scope("gather_trials_z"):
        up, down = [plane], [plane]
        for step in range(3):
            up.append(along_z(up[-1], 1))
            down.append(along_z(down[-1], -1))
        up[3], down[3], *turned = lax.optimization_barrier((up[3], down[3], *turned))
        far = [along_z(up[3][:1], 1), along_z(down[3][1:], -1)]
        gathered = [plane, down[1], down[2], down[3], far[0], up[3], up[2], up[1], far[1]]
        gathered = gathered + [swap_core(block) for block in gathered]
    with jax.named_scope("gather_conduction"):
        blocks = [pair, *turned]
        blocks = blocks + [swap_core(block) for block in blocks]

    with jax.named_scope("apply"):
        pieces = apply_both(place, gathered, blocks, valence_factor, screened)
    with jax.named_scope("reduce_row"):
        pieces = [part + swap_core(rest) for part, rest in zip(pieces[:2], pieces[2:])]
        total = exchange(jnp.stack(pieces, axis=1), ("y", "xh")).sum(axis=0)
    with jax.named_scope("reduce_col"):
        total = total.reshape(2, 64, 16, 32).transpose(2, 3, 0, 1).reshape(16, 32, 128)
        term = exchange(total, COL).sum(axis=0)
        kernel_term = term.reshape(32, 2, 64).transpose(1, 0, 2)
    differences = conduction_energy[None, :] - valence_energy[:, None]
    return differences[None] * trials - kernel_term


def solution(mesh):
    grid = Mesh(mesh.devices.reshape(4, 2, 2, 8, 2), ROW + COL)
    in_specs = (
        P(None, COL, ROW),
        P(ROW, None),
        P(COL, ROW),
        P(ROW, COL),
        P(COL),
        P(ROW),
    )
    out_specs = P(None, COL, ROW)
    return jax.shard_map(body, mesh=grid, in_specs=in_specs, out_specs=out_specs, check_vma=False)
```
